256 devices in a mesh: cand: 32 (over x, z_hi, core), tp: 8 (over y, z_lo).
Axes of the slice: x: 4, y: 4, z: 8 (z_hi: 4, z_lo: 2; z = z_hi * 2 + z_lo), core: 2. Of those that a mesh axis runs over, the one named last changes fastest.
Arguments:
- hidden_in: bfloat16 [256, 2, 8192], P('cand'), may hold values from -4 to 4
- queries: bfloat16 [256, 2, 32, 128], P('cand', None, 'tp'), may hold values from -128 to 128
- new_kv: bfloat16 [256, 2, 8, 2, 128], P('cand', None, 'tp'), may hold values from -5 to 5
- kv_cache: bfloat16 [256, 8, 2, 512, 128], P('cand', 'tp'), may hold values from -6 to 6
- lengths: int32 [256], P('cand'), may hold values from 128 to 512, as said below
- winner: int32 [8], replicated, may hold values from 0 to 31
- out_values: bfloat16 [4096, 8192], P('tp'), may hold values from -4 to 4
- out_scales: float32 [32, 64], P('tp'), may hold values from 0.008 to 0.032
Outputs:
- mixed: bfloat16 [256, 2, 8192], P('cand')
The draws below stay inside these ranges and needn't reach their ends.
Inputs may be any that keep to these rules, and one draw needn't show every extreme that they name: `lengths`: every draw has some row with exactly 512 live slots.
All inputs are finite; a program needn't handle non-finite values.
Results may differ from the reference program's by a relative error of at most 0.013.
Values may be sent and summed in bfloat16 or wider, within the bound.
No kernel may reach another device: no remote copies, remote signals or barrier semaphores. Data moves between devices by JAX's collectives and lax.ppermute only.
A program may use at most 64 MiB of HBM per device.

```python
import math
import jax
import jax.numpy as jnp
from jax import lax

D = 8192
H = 32
KVH = 8
HD = 128
PROB = 8
CACHE = 512
BLOCK = 64
STEPS = 2
SB = 128
ROWS = 256
N_CAND = 32


def draw_kv_cache(key, part):
    shape = (ROWS, KVH, 2, CACHE, HD)
    filled = jnp.clip(jax.random.normal(jax.random.fold_in(key, 502), shape, jnp.float32), -5.0, 5.0)
    return filled.astype(jnp.bfloat16)


def draw_queries(key, part):
    shape = (ROWS, STEPS, H, HD)
    entries = jnp.clip(2.0 * jax.random.normal(jax.random.fold_in(key, 503), shape, jnp.float32), -12.0, 12.0)
    return entries.astype(jnp.bfloat16)


def draw_lengths(key, part):
    devices_count = ROWS // PROB
    tier = jax.random.randint(jax.random.fold_in(key, 506), (devices_count,), 1, 5)
    ceiling = jnp.maximum(2 * BLOCK, CACHE * tier // 4)
    per_row = jnp.repeat(ceiling, PROB)
    drawn = jax.random.randint(jax.random.fold_in(key, 507), (ROWS,), 2 * BLOCK, per_row + 1)
    longest = jax.random.randint(jax.random.fold_in(key, 508), (), 0, ROWS)
    return jnp.where(jnp.arange(ROWS) == longest, CACHE, drawn).astype(jnp.int32)


def place_ends(array, own_key, low, largest):
    longest = array.shape.index(max(array.shape))
    spots = []
    for shift in (0, 1):
        where = [jax.random.randint(jax.random.fold_in(own_key, axis), (), 0, length) for axis, length in enumerate(array.shape)]
        where[longest] = (where[longest] + shift) % array.shape[longest]
        spots.append(tuple(where))
    return array.at[spots[0]].set(low).at[spots[1]].set(largest)


def block_scale(stream_key, extent, shards, least, high):
    def one(dim, parts):
        steps = jax.random.uniform(jax.random.fold_in(jax.random.fold_in(stream_key, 6), dim), (parts,), jnp.float32, least / len(shards), high / len(shards))
        return jnp.repeat(jnp.exp(steps), extent[dim] // parts).reshape((-1,) + (1,) * (len(extent) - dim - 1))

    level = one(*shards[0])
    for cut in shards[1:]:
        level = level * one(*cut)
    return level


def scatter_about(rng, extent, width, reach, pieces=(), held_as=jnp.bfloat16):
    level = block_scale(rng, extent, pieces, -0.22, 0.18) if pieces else 1.0
    values = jax.random.normal(rng, extent, jnp.float32) * width * level
    return jnp.minimum(jnp.maximum(values, -reach), reach).astype(held_as)


def setup_inputs(seed: int = 0) -> dict:
    arg_keys = jax.random.split(jax.random.key(seed), 9)
    return {
        "hidden_in": scatter_about(arg_keys[0], (ROWS, STEPS, D), 0.5, 4.0, ((0, 32),)),
        "queries": draw_queries(jax.random.fold_in(arg_keys[8], 71), 0),
        "new_kv": scatter_about(arg_keys[2], (ROWS, STEPS, KVH, 2, HD), 1.0, 5.0, ((0, 32), (2, 8))),
        "kv_cache": draw_kv_cache(jax.random.fold_in(arg_keys[8], 71), 0),
        "lengths": draw_lengths(jax.random.fold_in(arg_keys[8], 71), 0),
        "winner": place_ends(jax.random.randint(arg_keys[5], (PROB,), 0, N_CAND), jax.random.fold_in(arg_keys[5], 1), 0, N_CAND - 1).astype(jnp.int32),
        "out_values": scatter_about(arg_keys[6], (H * HD, D), 1.0, 4.0, ((0, 8),)),
        "out_scales": jnp.clip(jnp.exp(math.log(0.032) - 1.3862944 * jax.random.uniform(arg_keys[7], (H * HD // SB, D // SB), jnp.float32) ** block_scale(arg_keys[7], (H * HD // SB, D // SB), ((0, 8),), -0.2, 0.2)), 0.008, 0.032),
    }


def reference(hidden_in, queries, new_kv, kv_cache, lengths, winner, out_values, out_scales):
    group = H // KVH
    factor = 1.0 / math.sqrt(HD)
    positions = jnp.arange(CACHE, dtype=jnp.int32)
    causal = jnp.arange(STEPS, dtype=jnp.int32)[None, :] <= jnp.arange(STEPS, dtype=jnp.int32)[:, None]

    def one_row(row):
        problem = row % PROB
        source = winner[problem] * PROB + problem
        src_len = lengths[source]
        own_len = lengths[row]
        block = lax.dynamic_slice_in_dim(kv_cache[source], (src_len - BLOCK).astype(jnp.int32), BLOCK, 2)
        cache = lax.dynamic_update_slice_in_dim(kv_cache[row], block, (own_len - BLOCK).astype(jnp.int32), 2)
        query = queries[row].astype(jnp.float32).reshape(STEPS, KVH, group, HD)
        fresh = jnp.transpose(new_kv[row], (1, 2, 0, 3))
        keys = jnp.concatenate([cache[:, 0], fresh[:, 0]], axis=1).astype(jnp.float32)
        values = jnp.concatenate([cache[:, 1], fresh[:, 1]], axis=1).astype(jnp.float32)
        scores = jnp.einsum('tkgd,kjd->tkgj', query, keys) * factor
        old_valid = jnp.broadcast_to(positions[None, :] < own_len, (STEPS, CACHE))
        valid = jnp.concatenate([old_valid, causal], axis=1)
        scores = jnp.where(valid[:, None, None, :], scores, -jnp.inf)
        peak = lax.optimization_barrier(jnp.max(scores, axis=-1, keepdims=True))
        expo = jnp.exp(scores - peak)
        weights = (expo / lax.optimization_barrier(jnp.sum(expo, axis=-1, keepdims=True))).astype(jnp.bfloat16)
        attended = jnp.einsum('tkgj,kjd->tkgd', weights.astype(jnp.float32), values)
        return attended.astype(jnp.bfloat16).reshape(STEPS, H * HD)
    attended = lax.map(one_row, jnp.arange(ROWS, dtype=jnp.int32))
    flat = attended.reshape(ROWS * STEPS, H * HD)

    def add_block(index, term):
        piece = lax.dynamic_slice_in_dim(flat, index * SB, SB, 1)
        weight_rows = lax.dynamic_slice_in_dim(out_values, index * SB, SB, 0)
        scale = jnp.repeat(lax.dynamic_index_in_dim(out_scales, index, 0, keepdims=False), SB)
        return term + jnp.dot(piece, weight_rows, preferred_element_type=jnp.float32) * scale[None, :]
    term = lax.fori_loop(0, H * HD // SB, add_block, jnp.zeros((ROWS * STEPS, D), jnp.float32))
    result = (hidden_in.reshape(ROWS * STEPS, D).astype(jnp.float32) + term).astype(jnp.bfloat16)
    return result.reshape(ROWS, STEPS, D)
```

```python
import functools
import math

import jax
import jax.numpy as jnp
from jax import lax
from jax.experimental import pallas as pl
from jax.experimental.pallas import tpu as pltpu
from jax.sharding import PartitionSpec as P

BLOCK = 64
WINDOW = 80
CHUNK = 1024
VMEM = pl.BlockSpec(memory_space=pltpu.VMEM)
SMEM = pl.BlockSpec(memory_space=pltpu.SMEM)
ANY = pl.BlockSpec(memory_space=pl.ANY)
NT = (((1,), (1,)), ((), ()))


def exchange(x, axis, size, bit):
    return lax.ppermute(x, axis, [(i, i ^ bit) for i in range(size)])


def extract_kernel(lengths, winner, place, cache, keep, send, window, sems):
    problems = cache.shape[0]
    half = problems // 2

    def start_of(p):
        first = lengths[p] - BLOCK
        start = jnp.minimum((first // 16) * 16, cache.shape[3] - WINDOW)
        return pl.multiple_of(start, 16), first - start

    copies = []
    for p in range(problems):
        start, _ = start_of(p)
        copies.append(
            pltpu.make_async_copy(cache.at[p, 0, :, pl.ds(start, WINDOW), :], window.at[p], sems.at[p])
        )
        copies[-1].start()
    for p in range(problems):
        copies[p].wait()
    rows = lax.broadcasted_iota(jnp.int32, (16, 128), 0)
    for j in range(problems):
        p = j ^ (place[1] * half)
        _, offset = start_of(p)
        mine = winner[p] == place[0]
        where = (keep if j < half else send, j % half)
        for kv in range(2):
            head = jnp.where(
                rows < offset,
                window[p, kv, 64:80, :].astype(jnp.float32),
                window[p, kv, 0:16, :].astype(jnp.float32),
            )
            head = jnp.where(mine, head, 0.0).astype(jnp.bfloat16)
            tail = window[p, kv, 16:64, :].astype(jnp.float32)
            tail = jnp.where(mine, tail, 0.0).astype(jnp.bfloat16)
            base = where[1] * BLOCK
            where[0][kv, base : base + 16, :] = head
            where[0][kv, base + 16 : base + BLOCK, :] = tail


def old_kernel(lengths, queries, new_keys, new_values, cache, out, peak, total, held, sems, *, factor):
    problems = cache.shape[0]
    group = queries.shape[1] // 2
    copies = []
    for p in range(problems):
        copies.append(pltpu.make_async_copy(cache.at[p, 0], held.at[p], sems.at[p]))
        copies[-1].start()
    slots = lax.broadcasted_iota(jnp.int32, (queries.shape[1], cache.shape[3]), 1)
    later = lax.broadcasted_iota(jnp.int32, (queries.shape[1], 1), 0) >= group
    for p in range(problems):
        query = queries[p]
        wide = query.astype(jnp.float32)
        keys = [new_keys[p, u : u + 1, :].astype(jnp.float32) for u in range(2)]
        fresh = [jnp.sum(wide * key, -1, keepdims=True) * factor for key in keys]
        fresh[1] = jnp.where(later, fresh[1], -jnp.inf)
        copies[p].wait()
        scores = lax.dot_general(query, held[p, 0], NT, preferred_element_type=jnp.float32) * factor
        scores = jnp.where(slots < lengths[p] - BLOCK, scores, -jnp.inf)
        top = jnp.maximum(jnp.max(scores, -1, keepdims=True), jnp.maximum(fresh[0], fresh[1]))
        weights = jnp.exp(scores - top)
        sums = jnp.sum(weights, -1, keepdims=True)
        mixed = jnp.dot(weights.astype(jnp.bfloat16), held[p, 1], preferred_element_type=jnp.float32)
        for u in range(2):
            weight = jnp.exp(fresh[u] - top)
            sums = sums + weight
            mixed = mixed + weight * new_values[p, u : u + 1, :].astype(jnp.float32)
        out[p] = mixed
        peak[p] = jnp.broadcast_to(top, mixed.shape)
        total[p] = jnp.broadcast_to(sums, mixed.shape)


def start_weights(weights, held, sems, base):
    chunks = held.shape[1] // CHUNK
    copies = []
    for c in range(chunks):
        columns = pl.multiple_of(base + c * CHUNK, CHUNK)
        copies.append(
            pltpu.make_async_copy(
                weights.at[:, pl.ds(columns, CHUNK)], held.at[:, c * CHUNK : (c + 1) * CHUNK], sems.at[c]
            )
        )
        copies[-1].start()
    return copies


def project(attended, scales, held, copies, base, out):
    blocks, side = scales.shape[0], held.shape[0] // scales.shape[0]
    parts = [attended[pl.ds(b, 16, stride=blocks), :].astype(jnp.bfloat16) for b in range(blocks)]
    first = base // 128
    for c, copy in enumerate(copies):
        copy.wait()
        columns = slice(c * CHUNK, (c + 1) * CHUNK)
        terms = [
            jnp.dot(parts[b], held[b * side : (b + 1) * side, columns], preferred_element_type=jnp.float32)
            for b in range(blocks)
        ]
        for n in range(CHUNK // 128):
            block = first + c * (CHUNK // 128) + n
            sums = 0.0
            for b in range(blocks):
                sums = sums + terms[b][:, n * 128 : (n + 1) * 128] * scales[b, block]
            out[:, c * CHUNK + n * 128 : c * CHUNK + (n + 1) * 128] = sums.astype(out.dtype)


def fork_kernel(place, queries, mine, other, old, peak, total, scales, weights, attended, out, held, sems, *, factor):
    width = held.shape[1]
    base = (1 - place[2]) * width
    copies = start_weights(weights, held, sems, base)
    rows, keys_here = queries.shape[0], mine.shape[1]
    per_row = rows // (2 * keys_here // BLOCK)
    halves = []
    for half, ref in ((place[1], mine), (1 - place[1], other)):
        scores = lax.dot_general(queries[...], ref[0], NT, preferred_element_type=jnp.float32) * factor
        row = lax.broadcasted_iota(jnp.int32, scores.shape, 0) // per_row
        owner = lax.broadcasted_iota(jnp.int32, scores.shape, 1) // BLOCK + half * (keys_here // BLOCK)
        halves.append(jnp.where(row == owner, scores, -jnp.inf))
    top = jnp.maximum(jnp.max(halves[0], -1, keepdims=True), jnp.max(halves[1], -1, keepdims=True))
    top = jnp.maximum(peak[...], top)
    kept = jnp.exp(peak[...] - top)
    sums = total[...] * kept
    mixed = old[...] * kept
    for scores, ref in zip(halves, (mine, other)):
        share = jnp.exp(scores - top[:, :1])
        sums = sums + jnp.sum(share, -1, keepdims=True)
        mixed = mixed + jnp.dot(share.astype(jnp.bfloat16), ref[1], preferred_element_type=jnp.float32)
    attended[...] = (mixed / sums).astype(jnp.bfloat16).astype(jnp.float32)
    project(attended, scales, held, copies, base, out)


def project_kernel(place, attended, scales, weights, out, held, sems):
    base = place[2] * held.shape[1]
    copies = start_weights(weights, held, sems, base)
    project(attended, scales, held, copies, base, out)


def params(mib, flops, size):
    return dict(
        compiler_params=pltpu.CompilerParams(vmem_limit_bytes=mib * 2**20),
        cost_estimate=pl.CostEstimate(flops=flops, bytes_accessed=size, transcendentals=0),
    )


def local(hidden_in, queries, new_kv, kv_cache, lengths, winner, out_values, out_scales):
    problems, _, _, slots, head_dim = kv_cache.shape
    steps, heads = queries.shape[1], queries.shape[2]
    width = out_values.shape[1]
    factor = 1.0 / math.sqrt(head_dim)
    cand, tp = lax.axis_index("cand"), lax.axis_index("tp")
    place = jnp.stack([cand, cand % 2, tp % 2]).astype(jnp.int32)
    half = width // 2
    bf16, f32 = jnp.bfloat16, jnp.float32

    fork_shape = jax.ShapeDtypeStruct((2, problems // 2 * BLOCK, head_dim), bf16)
    keep, send = pl.pallas_call(
        extract_kernel,
        out_shape=(fork_shape, fork_shape),
        in_specs=[SMEM, SMEM, SMEM, ANY],
        out_specs=(VMEM, VMEM),
        scratch_shapes=[
            pltpu.VMEM((problems, 2, WINDOW, head_dim), bf16),
            pltpu.SemaphoreType.DMA((problems,)),
        ],
        **params(4, 0, 2**19),
    )(lengths, winner, place, kv_cache)

    grouped = queries.reshape(problems, steps * heads, head_dim)
    rows = problems * steps * heads
    partial = jax.ShapeDtypeStruct((problems, steps * heads, head_dim), f32)
    old, peak, total = pl.pallas_call(
        functools.partial(old_kernel, factor=factor),
        out_shape=(partial,) * 3,
        in_specs=[SMEM, VMEM, VMEM, VMEM, ANY],
        out_specs=(VMEM,) * 3,
        scratch_shapes=[
            pltpu.VMEM((problems, 2, slots, head_dim), bf16),
            pltpu.SemaphoreType.DMA((problems,)),
        ],
        **params(8, 2**24, 2**21),
    )(lengths, grouped, new_kv[:, :, 0, 0], new_kv[:, :, 0, 1], kv_cache)

    block = keep + exchange(send, "cand", 32, 1)
    for bit in (8, 16, 2, 4):
        block = block + exchange(block, "cand", 32, bit)
    other = exchange(block, "cand", 32, 1)

    flat = (rows, head_dim)
    half_shape = jax.ShapeDtypeStruct((problems * steps, half), bf16)
    scratch = [pltpu.VMEM((out_values.shape[0], half), bf16), pltpu.SemaphoreType.DMA((half // CHUNK,))]
    attended, away = pl.pallas_call(
        functools.partial(fork_kernel, factor=factor),
        out_shape=(jax.ShapeDtypeStruct(flat, f32), half_shape),
        in_specs=[SMEM] + [VMEM] * 6 + [SMEM, ANY],
        out_specs=(VMEM, VMEM),
        scratch_shapes=scratch,
        **params(12, 2**26, 2**22),
    )(
        place,
        grouped.reshape(flat),
        block,
        other,
        old.reshape(flat),
        peak.reshape(flat),
        total.reshape(flat),
        out_scales,
        out_values,
    )
    arrived = exchange(away, "tp", 8, 1)
    home = pl.pallas_call(
        project_kernel,
        out_shape=half_shape,
        in_specs=[SMEM, VMEM, SMEM, ANY],
        out_specs=VMEM,
        scratch_shapes=scratch,
        **params(12, 2**26, 2**22),
    )(place, attended, out_scales, out_values)

    sums = home + arrived
    for bit in (2, 4):
        sums = sums + exchange(sums, "tp", 8, bit)
    residual = hidden_in.reshape(problems * steps, width)
    residual = lax.dynamic_slice_in_dim(residual, (tp % 2) * half, half, 1)
    mixed = (residual.astype(f32) + sums.astype(f32)).astype(bf16)
    neighbour = exchange(mixed, "tp", 8, 1)
    first = tp % 2 == 0
    result = jnp.concatenate(
        [jnp.where(first, mixed, neighbour), jnp.where(first, neighbour, mixed)], axis=1
    )
    return result.reshape(hidden_in.shape)


def solution(mesh):
    placed = (
        P("cand", None, None),
        P("cand", None, "tp", None),
        P("cand", None, "tp", None, None),
        P("cand", "tp", None, None, None),
        P("cand"),
        P(),
        P("tp", None),
        P("tp", None),
    )
    return jax.shard_map(
        local, mesh=mesh, in_specs=placed, out_specs=P("cand", None, None), check_vma=False
    )
```

```python
import functools
import math

import jax
import jax.numpy as jnp
from jax import lax
from jax.experimental import pallas as pl
from jax.experimental.pallas import tpu as pltpu
from jax.sharding import PartitionSpec as P

BLOCK = 64
WINDOW = 80
CHUNK = 1024
VMEM = pl.BlockSpec(memory_space=pltpu.VMEM)
SMEM = pl.BlockSpec(memory_space=pltpu.SMEM)
HBM = pl.BlockSpec(memory_space=pltpu.HBM)
NT = (((1,), (1,)), ((), ()))


def exchange(x, axis, size, bit):
    return lax.ppermute(x, axis, [(i, i ^ bit) for i in range(size)])


def extract_kernel(place, lengths_in, winner_in, cache, keep, send, lengths, winner, window, sems):
    problems = cache.shape[0]
    half = problems // 2
    small = [
        pltpu.make_async_copy(lengths_in, lengths, sems.at[problems]),
        pltpu.make_async_copy(winner_in, winner, sems.at[problems + 1]),
    ]
    for copy in small:
        copy.start()
    for copy in small:
        copy.wait()

    def start_of(p):
        first = lengths[p] - BLOCK
        start = jnp.minimum((first // 16) * 16, cache.shape[3] - WINDOW)
        return pl.multiple_of(start, 16), first - start

    copies = []
    for p in range(problems):
        start, _ = start_of(p)
        copies.append(
            pltpu.make_async_copy(cache.at[p, 0, :, pl.ds(start, WINDOW), :], window.at[p], sems.at[p])
        )
        copies[-1].start()
    for p in range(problems):
        copies[p].wait()
    rows = lax.broadcasted_iota(jnp.int32, (16, 128), 0)
    for j in range(problems):
        p = j ^ (place[1] * half)
        _, offset = start_of(p)
        mine = winner[p] == place[0]
        where = (keep if j < half else send, j % half)
        for kv in range(2):
            head = jnp.where(
                rows < offset,
                window[p, kv, 64:80, :].astype(jnp.float32),
                window[p, kv, 0:16, :].astype(jnp.float32),
            )
            head = jnp.where(mine, head, 0.0).astype(jnp.bfloat16)
            tail = window[p, kv, 16:64, :].astype(jnp.float32)
            tail = jnp.where(mine, tail, 0.0).astype(jnp.bfloat16)
            base = where[1] * BLOCK
            where[0][kv, base : base + 16, :] = head
            where[0][kv, base + 16 : base + BLOCK, :] = tail


def old_kernel(lengths, queries, new_keys, new_values, cache, out, peak, total, passed, held, sems, *, factor):
    problems = cache.shape[0]
    group = queries.shape[1] // 2
    copies = []
    for p in range(problems):
        copies.append(pltpu.make_async_copy(cache.at[p, 0], held.at[p], sems.at[p]))
        copies[-1].start()
    slots = lax.broadcasted_iota(jnp.int32, (queries.shape[1], cache.shape[3]), 1)
    later = lax.broadcasted_iota(jnp.int32, (queries.shape[1], 1), 0) >= group
    for p in range(problems):
        query = queries[p]
        wide = query.astype(jnp.float32)
        keys = [new_keys[p, u : u + 1, :].astype(jnp.float32) for u in range(2)]
        fresh = [jnp.sum(wide * key, -1, keepdims=True) * factor for key in keys]
        fresh[1] = jnp.where(later, fresh[1], -jnp.inf)
        copies[p].wait()
        scores = lax.dot_general(query, held[p, 0], NT, preferred_element_type=jnp.float32) * factor
        scores = jnp.where(slots < lengths[p] - BLOCK, scores, -jnp.inf)
        top = jnp.maximum(jnp.max(scores, -1, keepdims=True), jnp.maximum(fresh[0], fresh[1]))
        weights = jnp.exp(scores - top)
        sums = jnp.sum(weights, -1, keepdims=True)
        mixed = jnp.dot(weights.astype(jnp.bfloat16), held[p, 1], preferred_element_type=jnp.float32)
        for u in range(2):
            weight = jnp.exp(fresh[u] - top)
            sums = sums + weight
            mixed = mixed + weight * new_values[p, u : u + 1, :].astype(jnp.float32)
        passed[p] = query
        out[p] = mixed
        peak[p] = jnp.broadcast_to(top, mixed.shape)
        total[p] = jnp.broadcast_to(sums, mixed.shape)


def start_weights(scales_in, scales, weights, held, sems, base):
    chunks = held.shape[1] // CHUNK
    copies = [pltpu.make_async_copy(scales_in, scales, sems.at[chunks])]
    copies[0].start()
    for c in range(chunks):
        columns = pl.multiple_of(base + c * CHUNK, CHUNK)
        copies.append(
            pltpu.make_async_copy(
                weights.at[:, pl.ds(columns, CHUNK)], held.at[:, c * CHUNK : (c + 1) * CHUNK], sems.at[c]
            )
        )
        copies[-1].start()
    return copies


def project(attended, scales, held, copies, base, out):
    blocks, side = scales.shape[0], held.shape[0] // scales.shape[0]
    parts = [attended[pl.ds(b, 16, stride=blocks), :].astype(jnp.bfloat16) for b in range(blocks)]
    first = base // 128
    copies[0].wait()
    for c, copy in enumerate(copies[1:]):
        copy.wait()
        columns = slice(c * CHUNK, (c + 1) * CHUNK)
        terms = [
            jnp.dot(parts[b], held[b * side : (b + 1) * side, columns], preferred_element_type=jnp.float32)
            for b in range(blocks)
        ]
        for n in range(CHUNK // 128):
            block = first + c * (CHUNK // 128) + n
            sums = 0.0
            for b in range(blocks):
                sums = sums + terms[b][:, n * 128 : (n + 1) * 128] * scales[b, block]
            out[:, c * CHUNK + n * 128 : c * CHUNK + (n + 1) * 128] = sums.astype(out.dtype)


def fork_kernel(
    place, queries, mine, other, old, peak, total, scales_in, weights, attended, out, scales, held, sems, *, factor
):
    width = held.shape[1]
    base = (1 - place[2]) * width
    copies = start_weights(scales_in, scales, weights, held, sems, base)
    rows, keys_here = queries.shape[0], mine.shape[1]
    per_row = rows // (2 * keys_here // BLOCK)
    halves = []
    for half, ref in ((place[1], mine), (1 - place[1], other)):
        scores = lax.dot_general(queries[...], ref[0], NT, preferred_element_type=jnp.float32) * factor
        row = lax.broadcasted_iota(jnp.int32, scores.shape, 0) // per_row
        owner = lax.broadcasted_iota(jnp.int32, scores.shape, 1) // BLOCK + half * (keys_here // BLOCK)
        halves.append(jnp.where(row == owner, scores, -jnp.inf))
    top = jnp.maximum(jnp.max(halves[0], -1, keepdims=True), jnp.max(halves[1], -1, keepdims=True))
    top = jnp.maximum(peak[...], top)
    kept = jnp.exp(peak[...] - top)
    sums = total[...] * kept
    mixed = old[...] * kept
    for scores, ref in zip(halves, (mine, other)):
        share = jnp.exp(scores - top[:, :1])
        sums = sums + jnp.sum(share, -1, keepdims=True)
        mixed = mixed + jnp.dot(share.astype(jnp.bfloat16), ref[1], preferred_element_type=jnp.float32)
    attended[...] = (mixed / sums).astype(jnp.bfloat16).astype(jnp.float32)
    project(attended, scales, held, copies, base, out)


def project_kernel(place, attended, scales_in, weights, out, scales, held, sems):
    base = place[2] * held.shape[1]
    copies = start_weights(scales_in, scales, weights, held, sems, base)
    project(attended, scales, held, copies, base, out)


def params(mib, flops, size):
    return dict(
        compiler_params=pltpu.CompilerParams(vmem_limit_bytes=mib * 2**20),
        cost_estimate=pl.CostEstimate(flops=flops, bytes_accessed=size, transcendentals=0),
    )


def local(hidden_in, queries, new_kv, kv_cache, lengths, winner, out_values, out_scales):
    problems, _, _, slots, head_dim = kv_cache.shape
    steps, heads = queries.shape[1], queries.shape[2]
    width = out_values.shape[1]
    factor = 1.0 / math.sqrt(head_dim)
    cand, tp = lax.axis_index("cand"), lax.axis_index("tp")
    kv_cache, lengths_far, winner, out_values, out_scales = (
        pltpu.with_memory_space_constraint(x, pltpu.HBM) for x in (kv_cache, lengths, winner, out_values, out_scales)
    )
    place = jnp.stack([cand, cand % 2, tp % 2]).astype(jnp.int32)
    half = width // 2
    bf16, f32 = jnp.bfloat16, jnp.float32

    fork_shape = jax.ShapeDtypeStruct((2, problems // 2 * BLOCK, head_dim), bf16)
    keep, send = pl.pallas_call(
        extract_kernel,
        out_shape=(fork_shape, fork_shape),
        in_specs=[SMEM, HBM, HBM, HBM],
        out_specs=(VMEM, VMEM),
        scratch_shapes=[
            pltpu.SMEM((problems,), jnp.int32),
            pltpu.SMEM((problems,), jnp.int32),
            pltpu.VMEM((problems, 2, WINDOW, head_dim), bf16),
            pltpu.SemaphoreType.DMA((problems + 2,)),
        ],
        **params(4, 0, 2**19),
    )(place, lengths_far, winner, kv_cache)

    grouped = queries.reshape(problems, steps * heads, head_dim)
    rows = problems * steps * heads
    partial = jax.ShapeDtypeStruct((problems, steps * heads, head_dim), f32)
    partials = pl.pallas_call(
        functools.partial(old_kernel, factor=factor),
        out_shape=(partial,) * 3 + (jax.ShapeDtypeStruct(partial.shape, bf16),),
        in_specs=[SMEM, VMEM, VMEM, VMEM, HBM],
        out_specs=(VMEM,) * 4,
        scratch_shapes=[
            pltpu.VMEM((problems, 2, slots, head_dim), bf16),
            pltpu.SemaphoreType.DMA((problems,)),
        ],
        **params(8, 2**24, 2**21),
    )(lengths, grouped, new_kv[:, :, 0, 0], new_kv[:, :, 0, 1], kv_cache)

    block = keep + exchange(send, "cand", 32, 1)
    for bit in (8, 24, 2, 6):
        received = exchange(block, "cand", 32, bit)
        if bit == 8:
            received, partials = lax.optimization_barrier((received, partials))
        block = block + received
    old, peak, total, grouped = partials
    other = exchange(block, "cand", 32, 1)

    flat = (rows, head_dim)
    half_shape = jax.ShapeDtypeStruct((problems * steps, half), bf16)
    scratch = [
        pltpu.SMEM(out_scales.shape, f32),
        pltpu.VMEM((out_values.shape[0], half), bf16),
        pltpu.SemaphoreType.DMA((half // CHUNK + 1,)),
    ]
    attended, away = pl.pallas_call(
        functools.partial(fork_kernel, factor=factor),
        out_shape=(jax.ShapeDtypeStruct(flat, f32), half_shape),
        in_specs=[SMEM] + [VMEM] * 6 + [HBM, HBM],
        out_specs=(VMEM, VMEM),
        scratch_shapes=scratch,
        **params(12, 2**26, 2**22),
    )(
        place,
        grouped.reshape(flat),
        block,
        other,
        old.reshape(flat),
        peak.reshape(flat),
        total.reshape(flat),
        out_scales,
        out_values,
    )
    arrived = exchange(away, "tp", 8, 1)
    home = pl.pallas_call(
        project_kernel,
        out_shape=half_shape,
        in_specs=[SMEM, VMEM, HBM, HBM],
        out_specs=VMEM,
        scratch_shapes=scratch,
        **params(12, 2**26, 2**22),
    )(place, attended, out_scales, out_values)

    sums = home + arrived
    ahead, back, across = (exchange(sums, "tp", 8, bit) for bit in (2, 6, 4))
    residual = hidden_in.reshape(problems * steps, width)
    residual = lax.dynamic_slice_in_dim(residual, (tp % 2) * half, half, 1)
    pairs = (sums.astype(f32) + ahead.astype(f32)) + (back.astype(f32) + across.astype(f32))
    mixed = (residual.astype(f32) + pairs).astype(bf16)
    neighbour = exchange(mixed, "tp", 8, 1)
    first = tp % 2 == 0
    result = jnp.concatenate(
        [jnp.where(first, mixed, neighbour), jnp.where(first, neighbour, mixed)], axis=1
    )
    return result.reshape(hidden_in.shape)


def solution(mesh):
    placed = (
        P("cand", None, None),
        P("cand", None, "tp", None),
        P("cand", None, "tp", None, None),
        P("cand", "tp", None, None, None),
        P("cand"),
        P(),
        P("tp", None),
        P("tp", None),
    )
    return jax.shard_map(
        local, mesh=mesh, in_specs=placed, out_specs=P("cand", None, None), check_vma=False
    )
```

```python
import functools
import math

import jax
import jax.numpy as jnp
from jax import lax
from jax.experimental import pallas as pl
from jax.experimental.pallas import tpu as pltpu
from jax.sharding import PartitionSpec as P

BLOCK = 64
WINDOW = 80
CHUNK = 1024
VMEM = pl.BlockSpec(memory_space=pltpu.VMEM)
SMEM = pl.BlockSpec(memory_space=pltpu.SMEM)
HBM = pl.BlockSpec(memory_space=pltpu.HBM)
NT = (((1,), (1,)), ((), ()))


def exchange(x, axis, size, bit):
    return lax.ppermute(x, axis, [(i, i ^ bit) for i in range(size)])


def extract_kernel(place, lengths_in, winner_in, cache, keep, send, lengths, winner, window, sems):
    problems = cache.shape[0]
    half = problems // 2
    small = [
        pltpu.make_async_copy(lengths_in, lengths, sems.at[problems]),
        pltpu.make_async_copy(winner_in, winner, sems.at[problems + 1]),
    ]
    for copy in small:
        copy.start()
    for copy in small:
        copy.wait()

    def start_of(p):
        first = lengths[p] - BLOCK
        start = jnp.minimum((first // 16) * 16, cache.shape[3] - WINDOW)
        return pl.multiple_of(start, 16), first - start

    copies = []
    for p in range(problems):
        start, _ = start_of(p)
        copies.append(
            pltpu.make_async_copy(cache.at[p, 0, :, pl.ds(start, WINDOW), :], window.at[p], sems.at[p])
        )
        copies[-1].start()
    for p in range(problems):
        copies[p].wait()
    rows = lax.broadcasted_iota(jnp.int32, (16, 128), 0)
    for j in range(problems):
        p = j ^ (place[1] * half)
        _, offset = start_of(p)
        mine = winner[p] == place[0]
        where = (keep if j < half else send, j % half)
        for kv in range(2):
            head = jnp.where(
                rows < offset,
                window[p, kv, 64:80, :].astype(jnp.float32),
                window[p, kv, 0:16, :].astype(jnp.float32),
            )
            head = jnp.where(mine, head, 0.0).astype(jnp.bfloat16)
            tail = window[p, kv, 16:64, :].astype(jnp.float32)
            tail = jnp.where(mine, tail, 0.0).astype(jnp.bfloat16)
            base = where[1] * BLOCK
            where[0][kv, base : base + 16, :] = head
            where[0][kv, base + 16 : base + BLOCK, :] = tail


def old_kernel(lengths, queries, new_keys, new_values, cache, out, peak, total, passed, held, sems, *, factor):
    problems = cache.shape[0]
    group = queries.shape[1] // 2
    copies = []
    for p in range(problems):
        copies.append(pltpu.make_async_copy(cache.at[p, 0], held.at[p], sems.at[p]))
        copies[-1].start()
    slots = lax.broadcasted_iota(jnp.int32, (queries.shape[1], cache.shape[3]), 1)
    later = lax.broadcasted_iota(jnp.int32, (queries.shape[1], 1), 0) >= group
    for p in range(problems):
        query = queries[p]
        wide = query.astype(jnp.float32)
        keys = [new_keys[p, u : u + 1, :].astype(jnp.float32) for u in range(2)]
        fresh = [jnp.sum(wide * key, -1, keepdims=True) * factor for key in keys]
        fresh[1] = jnp.where(later, fresh[1], -jnp.inf)
        copies[p].wait()
        scores = lax.dot_general(query, held[p, 0], NT, preferred_element_type=jnp.float32) * factor
        scores = jnp.where(slots < lengths[p] - BLOCK, scores, -jnp.inf)
        top = jnp.maximum(jnp.max(scores, -1, keepdims=True), jnp.maximum(fresh[0], fresh[1]))
        weights = jnp.exp(scores - top)
        sums = jnp.sum(weights, -1, keepdims=True)
        mixed = jnp.dot(weights.astype(jnp.bfloat16), held[p, 1], preferred_element_type=jnp.float32)
        for u in range(2):
            weight = jnp.exp(fresh[u] - top)
            sums = sums + weight
            mixed = mixed + weight * new_values[p, u : u + 1, :].astype(jnp.float32)
        passed[p] = query
        out[p] = mixed
        peak[p] = jnp.broadcast_to(top, mixed.shape)
        total[p] = jnp.broadcast_to(sums, mixed.shape)


def fetch_kernel(far, near, sems):
    rows = far.shape[0] // sems.shape[0]
    copies = [
        pltpu.make_async_copy(far.at[pl.ds(i * rows, rows)], near.at[pl.ds(i * rows, rows)], sems.at[i])
        for i in range(sems.shape[0])
    ]
    for copy in copies:
        copy.start()
    for copy in copies:
        copy.wait()


def project(attended, scales, weights, base, out):
    blocks, side = scales.shape[0], weights.shape[0] // scales.shape[0]
    parts = [attended[pl.ds(b, 16, stride=blocks), :].astype(jnp.bfloat16) for b in range(blocks)]
    for c in range(out.shape[1] // CHUNK):
        columns = pl.ds(pl.multiple_of(base + c * CHUNK, CHUNK), CHUNK)
        terms = [
            jnp.dot(parts[b], weights[b * side : (b + 1) * side, columns], preferred_element_type=jnp.float32)
            for b in range(blocks)
        ]
        for n in range(CHUNK // 128):
            block = base // 128 + c * (CHUNK // 128) + n
            sums = terms[0][:, n * 128 : (n + 1) * 128] * scales[0, block]
            for b in range(1, blocks):
                sums = sums + terms[b][:, n * 128 : (n + 1) * 128] * scales[b, block]
            out[:, c * CHUNK + n * 128 : c * CHUNK + (n + 1) * 128] = sums.astype(out.dtype)


def fork_kernel(
    place, queries, mine, other, old, peak, total, scales_in, weights, attended, out, scales, sem, *, factor
):
    scales_copy = pltpu.make_async_copy(scales_in, scales, sem)
    scales_copy.start()
    rows, keys_here = queries.shape[0], mine.shape[1]
    per_row = rows // (2 * keys_here // BLOCK)
    halves = []
    for half, ref in ((place[1], mine), (1 - place[1], other)):
        scores = lax.dot_general(queries[...], ref[0], NT, preferred_element_type=jnp.float32) * factor
        row = lax.broadcasted_iota(jnp.int32, scores.shape, 0) // per_row
        owner = lax.broadcasted_iota(jnp.int32, scores.shape, 1) // BLOCK + half * (keys_here // BLOCK)
        halves.append(jnp.where(row == owner, scores, -jnp.inf))
    top = jnp.maximum(jnp.max(halves[0], -1, keepdims=True), jnp.max(halves[1], -1, keepdims=True))
    top = jnp.maximum(peak[...], top)
    kept = jnp.exp(peak[...] - top)
    sums = total[...] * kept
    mixed = old[...] * kept
    for scores, ref in zip(halves, (mine, other)):
        share = jnp.exp(scores - top[:, :1])
        sums = sums + jnp.sum(share, -1, keepdims=True)
        mixed = mixed + jnp.dot(share.astype(jnp.bfloat16), ref[1], preferred_element_type=jnp.float32)
    attended[...] = (mixed / sums).astype(jnp.bfloat16).astype(jnp.float32)
    scales_copy.wait()
    project(attended, scales, weights, (1 - place[2]) * out.shape[1], out)


def project_kernel(place, attended, scales_in, weights, out, scales, sem):
    scales_copy = pltpu.make_async_copy(scales_in, scales, sem)
    scales_copy.start()
    scales_copy.wait()
    project(attended, scales, weights, place[2] * out.shape[1], out)


def params(mib, flops, size):
    return dict(
        compiler_params=pltpu.CompilerParams(vmem_limit_bytes=mib * 2**20),
        cost_estimate=pl.CostEstimate(flops=flops, bytes_accessed=size, transcendentals=0),
    )


def local(hidden_in, queries, new_kv, kv_cache, lengths, winner, out_values, out_scales):
    problems, _, _, slots, head_dim = kv_cache.shape
    steps, heads = queries.shape[1], queries.shape[2]
    width = out_values.shape[1]
    factor = 1.0 / math.sqrt(head_dim)
    cand, tp = lax.axis_index("cand"), lax.axis_index("tp")
    far_cache, far_lengths, winner, far_values, far_scales = (
        pltpu.with_memory_space_constraint(x, pltpu.HBM) for x in (kv_cache, lengths, winner, out_values, out_scales)
    )
    place = jnp.stack([cand, cand % 2, tp % 2]).astype(jnp.int32)
    half = width // 2
    bf16, f32 = jnp.bfloat16, jnp.float32

    fork_shape = jax.ShapeDtypeStruct((2, problems // 2 * BLOCK, head_dim), bf16)
    keep, send = pl.pallas_call(
        extract_kernel,
        out_shape=(fork_shape, fork_shape),
        in_specs=[SMEM, HBM, HBM, HBM],
        out_specs=(VMEM, VMEM),
        scratch_shapes=[
            pltpu.SMEM((problems,), jnp.int32),
            pltpu.SMEM((problems,), jnp.int32),
            pltpu.VMEM((problems, 2, WINDOW, head_dim), bf16),
            pltpu.SemaphoreType.DMA((problems + 2,)),
        ],
        **params(4, 0, 2**19),
    )(place, far_lengths, winner, far_cache)

    def attend_old(queries, new_kv, lengths):
        grouped = queries.reshape(problems, steps * heads, head_dim)
        partial = jax.ShapeDtypeStruct(grouped.shape, f32)
        return pl.pallas_call(
            functools.partial(old_kernel, factor=factor),
            out_shape=(partial,) * 3 + (jax.ShapeDtypeStruct(partial.shape, bf16),),
            in_specs=[SMEM, VMEM, VMEM, VMEM, HBM],
            out_specs=(VMEM,) * 4,
            scratch_shapes=[
                pltpu.VMEM((problems, 2, slots, head_dim), bf16),
                pltpu.SemaphoreType.DMA((problems,)),
            ],
            **params(8, 2**24, 2**21),
        )(lengths, grouped, new_kv[:, :, 0, 0], new_kv[:, :, 0, 1], far_cache)

    def fetch_weights(weights):
        return pl.pallas_call(
            fetch_kernel,
            out_shape=jax.ShapeDtypeStruct(weights.shape, bf16),
            in_specs=[HBM],
            out_specs=VMEM,
            scratch_shapes=[pltpu.SemaphoreType.DMA((8,))],
            **params(12, 0, 2**24),
        )(weights)

    block = keep + exchange(send, "cand", 32, 1)
    block = block + exchange(block, "cand", 32, 8)
    far_values, block = lax.optimization_barrier((far_values, block))
    received, weights = lax.optimization_barrier((exchange(block, "cand", 32, 24), fetch_weights(far_values)))
    block = block + received
    queries, new_kv, lengths, block = lax.optimization_barrier((queries, new_kv, lengths, block))
    received, partials = lax.optimization_barrier(
        (exchange(block, "cand", 32, 2), attend_old(queries, new_kv, lengths))
    )
    block = block + received
    block = block + exchange(block, "cand", 32, 6)
    old, peak, total, grouped = partials
    other = exchange(block, "cand", 32, 1)

    weights = pltpu.with_memory_space_constraint(weights, pltpu.VMEM)
    flat = (problems * steps * heads, head_dim)
    half_shape = jax.ShapeDtypeStruct((problems * steps, half), bf16)
    scratch = [pltpu.SMEM(out_scales.shape, f32), pltpu.SemaphoreType.DMA]
    attended, away = pl.pallas_call(
        functools.partial(fork_kernel, factor=factor),
        out_shape=(jax.ShapeDtypeStruct(flat, f32), half_shape),
        in_specs=[SMEM] + [VMEM] * 6 + [HBM, VMEM],
        out_specs=(VMEM, VMEM),
        scratch_shapes=scratch,
        **params(14, 2**26, 2**22),
    )(
        place,
        grouped.reshape(flat),
        block,
        other,
        old.reshape(flat),
        peak.reshape(flat),
        total.reshape(flat),
        far_scales,
        weights,
    )
    arrived = exchange(away, "tp", 8, 1)
    home = pl.pallas_call(
        project_kernel,
        out_shape=half_shape,
        in_specs=[SMEM, VMEM, HBM, VMEM],
        out_specs=VMEM,
        scratch_shapes=scratch,
        **params(14, 2**26, 2**22),
    )(place, attended, far_scales, weights)

    sums = home + arrived
    ahead, back, across = (exchange(sums, "tp", 8, bit) for bit in (2, 6, 4))
    residual = hidden_in.reshape(problems * steps, width)
    residual = lax.dynamic_slice_in_dim(residual, (tp % 2) * half, half, 1)
    pairs = (sums.astype(f32) + ahead.astype(f32)) + (back.astype(f32) + across.astype(f32))
    mixed = (residual.astype(f32) + pairs).astype(bf16)
    neighbour = exchange(mixed, "tp", 8, 1)
    first = tp % 2 == 0
    result = jnp.concatenate(
        [jnp.where(first, mixed, neighbour), jnp.where(first, neighbour, mixed)], axis=1
    )
    return result.reshape(hidden_in.shape)


def solution(mesh):
    placed = (
        P("cand", None, None),
        P("cand", None, "tp", None),
        P("cand", None, "tp", None, None),
        P("cand", "tp", None, None, None),
        P("cand"),
        P(),
        P("tp", None),
        P("tp", None),
    )
    return jax.shard_map(
        local, mesh=mesh, in_specs=placed, out_specs=P("cand", None, None), check_vma=False
    )
```

```python
import functools
import math

import jax
import jax.numpy as jnp
from jax import lax
from jax.experimental import pallas as pl
from jax.experimental.pallas import tpu as pltpu
from jax.sharding import PartitionSpec as P

BLOCK = 64
WINDOW = 80
CHUNK = 1024
VMEM = pl.BlockSpec(memory_space=pltpu.VMEM)
SMEM = pl.BlockSpec(memory_space=pltpu.SMEM)
HBM = pl.BlockSpec(memory_space=pltpu.HBM)
NT = (((1,), (1,)), ((), ()))


def exchange(x, axis, size, bit):
    return lax.ppermute(x, axis, [(i, i ^ bit) for i in range(size)])


def extract_kernel(place, lengths_in, winner_in, cache, keep, send, lengths, winner, window, sems):
    problems = cache.shape[0]
    half = problems // 2
    small = [
        pltpu.make_async_copy(lengths_in, lengths, sems.at[problems]),
        pltpu.make_async_copy(winner_in, winner, sems.at[problems + 1]),
    ]
    for copy in small:
        copy.start()
    for copy in small:
        copy.wait()

    def start_of(p):
        first = lengths[p] - BLOCK
        start = jnp.minimum((first // 16) * 16, cache.shape[3] - WINDOW)
        return pl.multiple_of(start, 16), first - start

    copies = []
    for p in range(problems):
        start, _ = start_of(p)
        copies.append(
            pltpu.make_async_copy(cache.at[p, 0, :, pl.ds(start, WINDOW), :], window.at[p], sems.at[p])
        )
        copies[-1].start()
    for p in range(problems):
        copies[p].wait()
    rows = lax.broadcasted_iota(jnp.int32, (16, 128), 0)
    for j in range(problems):
        p = j ^ (place[1] * half)
        _, offset = start_of(p)
        mine = winner[p] == place[0]
        where = (keep if j < half else send, j % half)
        for kv in range(2):
            head = jnp.where(
                rows < offset,
                window[p, kv, 64:80, :].astype(jnp.float32),
                window[p, kv, 0:16, :].astype(jnp.float32),
            )
            head = jnp.where(mine, head, 0.0).astype(jnp.bfloat16)
            tail = window[p, kv, 16:64, :].astype(jnp.float32)
            tail = jnp.where(mine, tail, 0.0).astype(jnp.bfloat16)
            base = where[1] * BLOCK
            where[0][kv, base : base + 16, :] = head
            where[0][kv, base + 16 : base + BLOCK, :] = tail


def old_kernel(
    lengths_in, queries_in, fresh_in, cache, out, peak, total, passed, lengths, fresh, held, sems, *, first, factor
):
    problems = out.shape[0]
    group = passed.shape[1] // 2
    copies = [
        pltpu.make_async_copy(lengths_in, lengths, sems.at[problems]),
        pltpu.make_async_copy(queries_in.at[first : first + problems], passed, sems.at[problems + 1]),
        pltpu.make_async_copy(fresh_in.at[first : first + problems], fresh, sems.at[problems + 2]),
    ]
    for copy in copies:
        copy.start()
    for i in range(problems):
        copies.append(pltpu.make_async_copy(cache.at[first + i, 0], held.at[i], sems.at[i]))
        copies[-1].start()
    slots = lax.broadcasted_iota(jnp.int32, (2 * group, cache.shape[3]), 1)
    later = lax.broadcasted_iota(jnp.int32, (2 * group, 1), 0) >= group
    for copy in copies:
        copy.wait()
    for i in range(problems):
        query = passed[i]
        wide = query.astype(jnp.float32)
        keys = [fresh[i, 2 * u : 2 * u + 1, :].astype(jnp.float32) for u in range(2)]
        values = [fresh[i, 2 * u + 1 : 2 * u + 2, :].astype(jnp.float32) for u in range(2)]
        new = [jnp.sum(wide * key, -1, keepdims=True) * factor for key in keys]
        new[1] = jnp.where(later, new[1], -jnp.inf)
        scores = lax.dot_general(query, held[i, 0], NT, preferred_element_type=jnp.float32) * factor
        scores = jnp.where(slots < lengths[first + i] - BLOCK, scores, -jnp.inf)
        top = jnp.maximum(jnp.max(scores, -1, keepdims=True), jnp.maximum(new[0], new[1]))
        weights = jnp.exp(scores - top)
        sums = jnp.sum(weights, -1, keepdims=True)
        mixed = jnp.dot(weights.astype(jnp.bfloat16), held[i, 1], preferred_element_type=jnp.float32)
        for u in range(2):
            weight = jnp.exp(new[u] - top)
            sums = sums + weight
            mixed = mixed + weight * values[u]
        out[i] = mixed
        peak[i] = jnp.broadcast_to(top, mixed.shape)
        total[i] = jnp.broadcast_to(sums, mixed.shape)


def fetch_kernel(place, far, near, sems, *, own):
    rows = far.shape[0] // sems.shape[0]
    half = place[2] if own else 1 - place[2]
    columns = pl.ds(pl.multiple_of(half * near.shape[1], 128), near.shape[1])
    copies = [
        pltpu.make_async_copy(far.at[pl.ds(i * rows, rows), columns], near.at[pl.ds(i * rows, rows)], sems.at[i])
        for i in range(sems.shape[0])
    ]
    for copy in copies:
        copy.start()
    for copy in copies:
        copy.wait()


def project(attended, scales, weights, base, out):
    blocks, side = scales.shape[0], weights.shape[0] // scales.shape[0]
    parts = [attended[pl.ds(b, 16, stride=blocks), :].astype(jnp.bfloat16) for b in range(blocks)]
    for c in range(out.shape[1] // CHUNK):
        columns = slice(c * CHUNK, (c + 1) * CHUNK)
        terms = [
            jnp.dot(parts[b], weights[b * side : (b + 1) * side, columns], preferred_element_type=jnp.float32)
            for b in range(blocks)
        ]
        for n in range(CHUNK // 128):
            block = base // 128 + c * (CHUNK // 128) + n
            sums = terms[0][:, n * 128 : (n + 1) * 128] * scales[0, block]
            for b in range(1, blocks):
                sums = sums + terms[b][:, n * 128 : (n + 1) * 128] * scales[b, block]
            out[:, c * CHUNK + n * 128 : c * CHUNK + (n + 1) * 128] = sums.astype(out.dtype)


def fork_kernel(place, mine, other, *refs, factor):
    parts, (scales_in, weights, attended, out, scales, sem) = refs[:8], refs[8:]
    scales_copy = pltpu.make_async_copy(scales_in, scales, sem)
    scales_copy.start()
    old, peak, total, queries = (jnp.concatenate([parts[i][...], parts[i + 4][...]], 0) for i in range(4))
    rows, keys_here = queries.shape[0], mine.shape[1]
    per_row = rows // (2 * keys_here // BLOCK)
    halves = []
    for half, ref in ((place[1], mine), (1 - place[1], other)):
        scores = lax.dot_general(queries, ref[0], NT, preferred_element_type=jnp.float32) * factor
        row = lax.broadcasted_iota(jnp.int32, scores.shape, 0) // per_row
        owner = lax.broadcasted_iota(jnp.int32, scores.shape, 1) // BLOCK + half * (keys_here // BLOCK)
        halves.append(jnp.where(row == owner, scores, -jnp.inf))
    top = jnp.maximum(jnp.max(halves[0], -1, keepdims=True), jnp.max(halves[1], -1, keepdims=True))
    top = jnp.maximum(peak, top)
    kept = jnp.exp(peak - top)
    sums = total * kept
    mixed = old * kept
    for scores, ref in zip(halves, (mine, other)):
        share = jnp.exp(scores - top[:, :1])
        sums = sums + jnp.sum(share, -1, keepdims=True)
        mixed = mixed + jnp.dot(share.astype(jnp.bfloat16), ref[1], preferred_element_type=jnp.float32)
    attended[...] = (mixed / sums).astype(jnp.bfloat16).astype(jnp.float32)
    scales_copy.wait()
    project(attended, scales, weights, (1 - place[2]) * out.shape[1], out)


def project_kernel(place, attended, scales_in, weights, out, scales, sem):
    scales_copy = pltpu.make_async_copy(scales_in, scales, sem)
    scales_copy.start()
    scales_copy.wait()
    project(attended, scales, weights, place[2] * out.shape[1], out)


def params(mib, flops, size):
    return dict(
        compiler_params=pltpu.CompilerParams(vmem_limit_bytes=mib * 2**20),
        cost_estimate=pl.CostEstimate(flops=flops, bytes_accessed=size, transcendentals=0),
    )


def local(hidden_in, queries, new_kv, kv_cache, lengths, winner, out_values, out_scales):
    problems, _, _, slots, head_dim = kv_cache.shape
    steps, heads = queries.shape[1], queries.shape[2]
    width = out_values.shape[1]
    factor = 1.0 / math.sqrt(head_dim)
    cand, tp = lax.axis_index("cand"), lax.axis_index("tp")
    far_cache, far_lengths, winner, far_values, far_scales = (
        pltpu.with_memory_space_constraint(x, pltpu.HBM) for x in (kv_cache, lengths, winner, out_values, out_scales)
    )
    place = jnp.stack([cand, cand % 2, tp % 2]).astype(jnp.int32)
    half = width // 2
    bf16, f32 = jnp.bfloat16, jnp.float32

    fork_shape = jax.ShapeDtypeStruct((2, problems // 2 * BLOCK, head_dim), bf16)
    keep, send = pl.pallas_call(
        extract_kernel,
        out_shape=(fork_shape, fork_shape),
        in_specs=[SMEM, HBM, HBM, HBM],
        out_specs=(VMEM, VMEM),
        scratch_shapes=[
            pltpu.SMEM((problems,), jnp.int32),
            pltpu.SMEM((problems,), jnp.int32),
            pltpu.VMEM((problems, 2, WINDOW, head_dim), bf16),
            pltpu.SemaphoreType.DMA((problems + 2,)),
        ],
        **params(4, 0, 2**19),
    )(place, far_lengths, winner, far_cache)

    def attend_old(queries, fresh, lengths, first):
        queries, fresh, lengths = (
            pltpu.with_memory_space_constraint(x, pltpu.HBM) for x in (queries, fresh, lengths)
        )
        partial = jax.ShapeDtypeStruct((problems // 2, steps * heads, head_dim), f32)
        return pl.pallas_call(
            functools.partial(old_kernel, first=first, factor=factor),
            out_shape=(partial,) * 3 + (jax.ShapeDtypeStruct(partial.shape, bf16),),
            in_specs=[HBM, HBM, HBM, HBM],
            out_specs=(VMEM,) * 4,
            scratch_shapes=[
                pltpu.SMEM(lengths.shape, jnp.int32),
                pltpu.VMEM((problems // 2, *fresh.shape[1:]), bf16),
                pltpu.VMEM((problems // 2, 2, slots, head_dim), bf16),
                pltpu.SemaphoreType.DMA((problems // 2 + 3,)),
            ],
            **params(8, 2**23, 2**20),
        )(lengths, queries, fresh, far_cache)

    def fetch_weights(weights, own):
        return pl.pallas_call(
            functools.partial(fetch_kernel, own=own),
            out_shape=jax.ShapeDtypeStruct((weights.shape[0], half), bf16),
            in_specs=[SMEM, HBM],
            out_specs=VMEM,
            scratch_shapes=[pltpu.SemaphoreType.DMA((8,))],
            **params(8, 0, 2**23),
        )(place, weights)

    block = keep + exchange(send, "cand", 32, 1)
    queries = queries.reshape(problems, steps * heads, head_dim)
    fresh = new_kv.reshape(problems, 2 * steps, head_dim)
    queries, fresh, lengths, block = lax.optimization_barrier((queries, fresh, lengths, block))
    received, part = lax.optimization_barrier(
        (exchange(block, "cand", 32, 8), attend_old(queries, fresh, lengths, 0))
    )
    block = block + received
    queries, fresh, lengths, block = lax.optimization_barrier((queries, fresh, lengths, block))
    received, rest = lax.optimization_barrier(
        (exchange(block, "cand", 32, 24), attend_old(queries, fresh, lengths, problems // 2))
    )
    block = block + received
    far_values, block = lax.optimization_barrier((far_values, block))
    received, away_weights = lax.optimization_barrier(
        (exchange(block, "cand", 32, 2), fetch_weights(far_values, False))
    )
    block = block + received
    far_values, block = lax.optimization_barrier((far_values, block))
    received, home_weights = lax.optimization_barrier(
        (exchange(block, "cand", 32, 6), fetch_weights(far_values, True))
    )
    block = block + received
    other = exchange(block, "cand", 32, 1)

    away_weights, home_weights = (
        pltpu.with_memory_space_constraint(x, pltpu.VMEM) for x in (away_weights, home_weights)
    )
    flat = (problems * steps * heads, head_dim)
    half_shape = jax.ShapeDtypeStruct((problems * steps, half), bf16)
    scratch = [pltpu.SMEM(out_scales.shape, f32), pltpu.SemaphoreType.DMA]
    attended, away = pl.pallas_call(
        functools.partial(fork_kernel, factor=factor),
        out_shape=(jax.ShapeDtypeStruct(flat, f32), half_shape),
        in_specs=[SMEM] + [VMEM] * 10 + [HBM, VMEM],
        out_specs=(VMEM, VMEM),
        scratch_shapes=scratch,
        **params(14, 2**26, 2**22),
    )(
        place,
        block,
        other,
        *(x.reshape(flat[0] // 2, head_dim) for x in (*part, *rest)),
        far_scales,
        away_weights,
    )
    arrived = exchange(away, "tp", 8, 1)
    home = pl.pallas_call(
        project_kernel,
        out_shape=half_shape,
        in_specs=[SMEM, VMEM, HBM, VMEM],
        out_specs=VMEM,
        scratch_shapes=scratch,
        **params(14, 2**26, 2**22),
    )(place, attended, far_scales, home_weights)

    sums = home + arrived
    ahead, back, across = (exchange(sums, "tp", 8, bit) for bit in (2, 6, 4))
    residual = hidden_in.reshape(problems * steps, width)
    residual = lax.dynamic_slice_in_dim(residual, (tp % 2) * half, half, 1)
    pairs = (sums.astype(f32) + ahead.astype(f32)) + (back.astype(f32) + across.astype(f32))
    mixed = (residual.astype(f32) + pairs).astype(bf16)
    neighbour = exchange(mixed, "tp", 8, 1)
    first = tp % 2 == 0
    result = jnp.concatenate(
        [jnp.where(first, mixed, neighbour), jnp.where(first, neighbour, mixed)], axis=1
    )
    return result.reshape(hidden_in.shape)


def solution(mesh):
    placed = (
        P("cand", None, None),
        P("cand", None, "tp", None),
        P("cand", None, "tp", None, None),
        P("cand", "tp", None, None, None),
        P("cand"),
        P(),
        P("tp", None),
        P("tp", None),
    )
    return jax.shard_map(
        local, mesh=mesh, in_specs=placed, out_specs=P("cand", None, None), check_vma=False
    )
```

```python
import functools
import math

import jax
import jax.numpy as jnp
from jax import lax
from jax.experimental import pallas as pl
from jax.experimental.pallas import tpu as pltpu
from jax.sharding import PartitionSpec as P

BLOCK = 64
WINDOW = 80
CHUNK = 1024
VMEM = pl.BlockSpec(memory_space=pltpu.VMEM)
SMEM = pl.BlockSpec(memory_space=pltpu.SMEM)
HBM = pl.BlockSpec(memory_space=pltpu.HBM)
NT = (((1,), (1,)), ((), ()))


def exchange(x, axis, size, bit):
    return lax.ppermute(x, axis, [(i, i ^ bit) for i in range(size)])


def extract_kernel(place, lengths_in, winner_in, cache, keep, send, lengths, winner, window, sems):
    problems = cache.shape[0]
    half = problems // 2
    small = [
        pltpu.make_async_copy(lengths_in, lengths, sems.at[problems]),
        pltpu.make_async_copy(winner_in, winner, sems.at[problems + 1]),
    ]
    for copy in small:
        copy.start()
    for copy in small:
        copy.wait()

    def start_of(p):
        first = lengths[p] - BLOCK
        start = jnp.minimum((first // 16) * 16, cache.shape[3] - WINDOW)
        return pl.multiple_of(start, 16), first - start

    copies = []
    for p in range(problems):
        start, _ = start_of(p)
        copies.append(
            pltpu.make_async_copy(cache.at[p, 0, :, pl.ds(start, WINDOW), :], window.at[p], sems.at[p])
        )
        copies[-1].start()
    for p in range(problems):
        copies[p].wait()
    rows = lax.broadcasted_iota(jnp.int32, (16, 128), 0)
    for j in range(problems):
        p = j ^ (place[1] * half + place[3] * (half // 2))
        _, offset = start_of(p)
        mine = winner[p] == place[0]
        where = (keep if j < half else send, j % half)
        for kv in range(2):
            head = jnp.where(
                rows < offset,
                window[p, kv, 64:80, :].astype(jnp.float32),
                window[p, kv, 0:16, :].astype(jnp.float32),
            )
            head = jnp.where(mine, head, 0.0).astype(jnp.bfloat16)
            tail = window[p, kv, 16:64, :].astype(jnp.float32)
            tail = jnp.where(mine, tail, 0.0).astype(jnp.bfloat16)
            base = where[1] * BLOCK
            where[0][kv, base : base + 16, :] = head
            where[0][kv, base + 16 : base + BLOCK, :] = tail


def old_kernel(
    lengths_in, queries_in, fresh_in, cache, out, peak, total, passed, lengths, fresh, held, sems, *, first, factor
):
    problems = out.shape[0]
    group = passed.shape[1] // 2
    copies = [
        pltpu.make_async_copy(lengths_in, lengths, sems.at[problems]),
        pltpu.make_async_copy(queries_in.at[first : first + problems], passed, sems.at[problems + 1]),
        pltpu.make_async_copy(fresh_in.at[first : first + problems], fresh, sems.at[problems + 2]),
    ]
    for copy in copies:
        copy.start()
    for i in range(problems):
        copies.append(pltpu.make_async_copy(cache.at[first + i, 0], held.at[i], sems.at[i]))
        copies[-1].start()
    slots = lax.broadcasted_iota(jnp.int32, (2 * group, cache.shape[3]), 1)
    later = lax.broadcasted_iota(jnp.int32, (2 * group, 1), 0) >= group
    for copy in copies:
        copy.wait()
    for i in range(problems):
        query = passed[i]
        wide = query.astype(jnp.float32)
        keys = [fresh[i, 2 * u : 2 * u + 1, :].astype(jnp.float32) for u in range(2)]
        values = [fresh[i, 2 * u + 1 : 2 * u + 2, :].astype(jnp.float32) for u in range(2)]
        new = [jnp.sum(wide * key, -1, keepdims=True) * factor for key in keys]
        new[1] = jnp.where(later, new[1], -jnp.inf)
        scores = lax.dot_general(query, held[i, 0], NT, preferred_element_type=jnp.float32) * factor
        scores = jnp.where(slots < lengths[first + i] - BLOCK, scores, -jnp.inf)
        top = jnp.maximum(jnp.max(scores, -1, keepdims=True), jnp.maximum(new[0], new[1]))
        weights = jnp.exp(scores - top)
        sums = jnp.sum(weights, -1, keepdims=True)
        mixed = jnp.dot(weights.astype(jnp.bfloat16), held[i, 1], preferred_element_type=jnp.float32)
        for u in range(2):
            weight = jnp.exp(new[u] - top)
            sums = sums + weight
            mixed = mixed + weight * values[u]
        out[i] = mixed
        peak[i] = jnp.broadcast_to(top, mixed.shape)
        total[i] = jnp.broadcast_to(sums, mixed.shape)


def fetch_kernel(place, far, near, sems, *, own):
    rows = far.shape[0] // sems.shape[0]
    half = place[2] if own else 1 - place[2]
    columns = pl.ds(pl.multiple_of(half * near.shape[1], 128), near.shape[1])
    copies = [
        pltpu.make_async_copy(far.at[pl.ds(i * rows, rows), columns], near.at[pl.ds(i * rows, rows)], sems.at[i])
        for i in range(sems.shape[0])
    ]
    for copy in copies:
        copy.start()
    for copy in copies:
        copy.wait()


def project(attended, scales, weights, base, out):
    blocks, side = scales.shape[0], weights.shape[0] // scales.shape[0]
    parts = [attended[pl.ds(b, 16, stride=blocks), :].astype(jnp.bfloat16) for b in range(blocks)]
    for c in range(out.shape[1] // CHUNK):
        columns = slice(c * CHUNK, (c + 1) * CHUNK)
        terms = [
            jnp.dot(parts[b], weights[b * side : (b + 1) * side, columns], preferred_element_type=jnp.float32)
            for b in range(blocks)
        ]
        for n in range(CHUNK // 128):
            block = base // 128 + c * (CHUNK // 128) + n
            sums = terms[0][:, n * 128 : (n + 1) * 128] * scales[0, block]
            for b in range(1, blocks):
                sums = sums + terms[b][:, n * 128 : (n + 1) * 128] * scales[b, block]
            out[:, c * CHUNK + n * 128 : c * CHUNK + (n + 1) * 128] = sums.astype(out.dtype)


def fork_kernel(place, mine, other, *refs, factor):
    parts, (scales_in, weights, attended, out, scales, sem) = refs[:8], refs[8:]
    scales_copy = pltpu.make_async_copy(scales_in, scales, sem)
    scales_copy.start()
    old, peak, total, queries = (jnp.concatenate([parts[i][...], parts[i + 4][...]], 0) for i in range(4))
    rows, keys_here = queries.shape[0], mine.shape[1]
    per_row = rows // (2 * keys_here // BLOCK)
    halves = []
    for half, ref in ((place[1], mine), (1 - place[1], other)):
        scores = lax.dot_general(queries, ref[0], NT, preferred_element_type=jnp.float32) * factor
        row = lax.broadcasted_iota(jnp.int32, scores.shape, 0) // per_row
        owner = lax.broadcasted_iota(jnp.int32, scores.shape, 1) // BLOCK
        owner = (owner ^ (place[3] * (keys_here // BLOCK // 2))) + half * (keys_here // BLOCK)
        halves.append(jnp.where(row == owner, scores, -jnp.inf))
    top = jnp.maximum(jnp.max(halves[0], -1, keepdims=True), jnp.max(halves[1], -1, keepdims=True))
    top = jnp.maximum(peak, top)
    kept = jnp.exp(peak - top)
    sums = total * kept
    mixed = old * kept
    for scores, ref in zip(halves, (mine, other)):
        share = jnp.exp(scores - top[:, :1])
        sums = sums + jnp.sum(share, -1, keepdims=True)
        mixed = mixed + jnp.dot(share.astype(jnp.bfloat16), ref[1], preferred_element_type=jnp.float32)
    attended[...] = (mixed / sums).astype(jnp.bfloat16).astype(jnp.float32)
    scales_copy.wait()
    project(attended, scales, weights, (1 - place[2]) * out.shape[1], out)


def project_kernel(place, attended, scales_in, weights, out, scales, sem):
    scales_copy = pltpu.make_async_copy(scales_in, scales, sem)
    scales_copy.start()
    scales_copy.wait()
    project(attended, scales, weights, place[2] * out.shape[1], out)


def params(mib, flops, size):
    return dict(
        compiler_params=pltpu.CompilerParams(vmem_limit_bytes=mib * 2**20),
        cost_estimate=pl.CostEstimate(flops=flops, bytes_accessed=size, transcendentals=0),
    )


def local(hidden_in, queries, new_kv, kv_cache, lengths, winner, out_values, out_scales):
    problems, _, _, slots, head_dim = kv_cache.shape
    steps, heads = queries.shape[1], queries.shape[2]
    width = out_values.shape[1]
    factor = 1.0 / math.sqrt(head_dim)
    cand, tp = lax.axis_index("cand"), lax.axis_index("tp")
    far_cache, far_lengths, winner, far_values, far_scales = (
        pltpu.with_memory_space_constraint(x, pltpu.HBM) for x in (kv_cache, lengths, winner, out_values, out_scales)
    )
    place = jnp.stack([cand, cand % 2, tp % 2, (cand // 8 + cand // 16) % 2]).astype(jnp.int32)
    half = width // 2
    bf16, f32 = jnp.bfloat16, jnp.float32

    fork_shape = jax.ShapeDtypeStruct((2, problems // 2 * BLOCK, head_dim), bf16)
    keep, send = pl.pallas_call(
        extract_kernel,
        out_shape=(fork_shape, fork_shape),
        in_specs=[SMEM, HBM, HBM, HBM],
        out_specs=(VMEM, VMEM),
        scratch_shapes=[
            pltpu.SMEM((problems,), jnp.int32),
            pltpu.SMEM((problems,), jnp.int32),
            pltpu.VMEM((problems, 2, WINDOW, head_dim), bf16),
            pltpu.SemaphoreType.DMA((problems + 2,)),
        ],
        **params(4, 0, 2**19),
    )(place, far_lengths, winner, far_cache)

    def attend_old(queries, fresh, lengths, first):
        queries, fresh, lengths = (
            pltpu.with_memory_space_constraint(x, pltpu.HBM) for x in (queries, fresh, lengths)
        )
        partial = jax.ShapeDtypeStruct((problems // 2, steps * heads, head_dim), f32)
        return pl.pallas_call(
            functools.partial(old_kernel, first=first, factor=factor),
            out_shape=(partial,) * 3 + (jax.ShapeDtypeStruct(partial.shape, bf16),),
            in_specs=[HBM, HBM, HBM, HBM],
            out_specs=(VMEM,) * 4,
            scratch_shapes=[
                pltpu.SMEM(lengths.shape, jnp.int32),
                pltpu.VMEM((problems // 2, *fresh.shape[1:]), bf16),
                pltpu.VMEM((problems // 2, 2, slots, head_dim), bf16),
                pltpu.SemaphoreType.DMA((problems // 2 + 3,)),
            ],
            **params(8, 2**23, 2**20),
        )(lengths, queries, fresh, far_cache)

    def fetch_weights(weights, own):
        return pl.pallas_call(
            functools.partial(fetch_kernel, own=own),
            out_shape=jax.ShapeDtypeStruct((weights.shape[0], half), bf16),
            in_specs=[SMEM, HBM],
            out_specs=VMEM,
            scratch_shapes=[pltpu.SemaphoreType.DMA((8,))],
            **params(8, 0, 2**23),
        )(place, weights)

    block = keep + exchange(send, "cand", 32, 1)
    queries = queries.reshape(problems, steps * heads, head_dim)
    fresh = new_kv.reshape(problems, 2 * steps, head_dim)
    middle = block.shape[1] // 2
    far_values, block = lax.optimization_barrier((far_values, block))
    received, home_weights = lax.optimization_barrier(
        (exchange(block[:, middle:], "cand", 32, 8), fetch_weights(far_values, True))
    )
    block = block[:, :middle] + received
    queries, fresh, lengths, block = lax.optimization_barrier((queries, fresh, lengths, block))
    received, part = lax.optimization_barrier(
        (exchange(block, "cand", 32, 24), attend_old(queries, fresh, lengths, 0))
    )
    block = block + received
    queries, fresh, lengths, block = lax.optimization_barrier((queries, fresh, lengths, block))
    received, rest = lax.optimization_barrier(
        (exchange(block, "cand", 32, 2), attend_old(queries, fresh, lengths, problems // 2))
    )
    block = block + received
    far_values, block = lax.optimization_barrier((far_values, block))
    received, away_weights = lax.optimization_barrier(
        (exchange(block, "cand", 32, 6), fetch_weights(far_values, False))
    )
    block = block + received
    received = exchange(block, "cand", 32, 8)
    block = jnp.concatenate([block, received], axis=1)
    other = exchange(block, "cand", 32, 1)

    away_weights, home_weights = (
        pltpu.with_memory_space_constraint(x, pltpu.VMEM) for x in (away_weights, home_weights)
    )
    flat = (problems * steps * heads, head_dim)
    half_shape = jax.ShapeDtypeStruct((problems * steps, half), bf16)
    scratch = [pltpu.SMEM(out_scales.shape, f32), pltpu.SemaphoreType.DMA]
    attended, away = pl.pallas_call(
        functools.partial(fork_kernel, factor=factor),
        out_shape=(jax.ShapeDtypeStruct(flat, f32), half_shape),
        in_specs=[SMEM] + [VMEM] * 10 + [HBM, VMEM],
        out_specs=(VMEM, VMEM),
        scratch_shapes=scratch,
        **params(14, 2**26, 2**22),
    )(
        place,
        block,
        other,
        *(x.reshape(flat[0] // 2, head_dim) for x in (*part, *rest)),
        far_scales,
        away_weights,
    )
    arrived = exchange(away, "tp", 8, 1)
    home = pl.pallas_call(
        project_kernel,
        out_shape=half_shape,
        in_specs=[SMEM, VMEM, HBM, VMEM],
        out_specs=VMEM,
        scratch_shapes=scratch,
        **params(14, 2**26, 2**22),
    )(place, attended, far_scales, home_weights)

    sums = home + arrived
    ahead, back, across = (exchange(sums, "tp", 8, bit) for bit in (2, 6, 4))
    residual = hidden_in.reshape(problems * steps, width)
    residual = lax.dynamic_slice_in_dim(residual, (tp % 2) * half, half, 1)
    pairs = (sums.astype(f32) + ahead.astype(f32)) + (back.astype(f32) + across.astype(f32))
    mixed = (residual.astype(f32) + pairs).astype(bf16)
    neighbour = exchange(mixed, "tp", 8, 1)
    first = tp % 2 == 0
    result = jnp.concatenate(
        [jnp.where(first, mixed, neighbour), jnp.where(first, neighbour, mixed)], axis=1
    )
    return result.reshape(hidden_in.shape)


def solution(mesh):
    placed = (
        P("cand", None, None),
        P("cand", None, "tp", None),
        P("cand", None, "tp", None, None),
        P("cand", "tp", None, None, None),
        P("cand"),
        P(),
        P("tp", None),
        P("tp", None),
    )
    return jax.shard_map(
        local, mesh=mesh, in_specs=placed, out_specs=P("cand", None, None), check_vma=False
    )
```

```python
import functools
import math

import jax
import jax.numpy as jnp
from jax import lax
from jax.experimental import pallas as pl
from jax.experimental.pallas import tpu as pltpu
from jax.sharding import PartitionSpec as P

BLOCK = 64
WINDOW = 80
CHUNK = 1024
VMEM = pl.BlockSpec(memory_space=pltpu.VMEM)
SMEM = pl.BlockSpec(memory_space=pltpu.SMEM)
HBM = pl.BlockSpec(memory_space=pltpu.HBM)
NT = (((1,), (1,)), ((), ()))


def exchange(x, axis, size, bit):
    return lax.ppermute(x, axis, [(i, i ^ bit) for i in range(size)])


def extract_kernel(place, lengths_in, winner_in, cache, keep, send, lengths, winner, window, sems):
    problems = cache.shape[0]
    half = problems // 2
    small = [
        pltpu.make_async_copy(lengths_in, lengths, sems.at[problems]),
        pltpu.make_async_copy(winner_in, winner, sems.at[problems + 1]),
    ]
    for copy in small:
        copy.start()
    for copy in small:
        copy.wait()

    def start_of(p):
        first = lengths[p] - BLOCK
        start = jnp.minimum((first // 16) * 16, cache.shape[3] - WINDOW)
        return pl.multiple_of(start, 16), first - start

    def window_copy(p):
        start, _ = start_of(p)
        return pltpu.make_async_copy(
            cache.at[p, 0, :, pl.ds(start, WINDOW), :], window.at[p], sems.at[p]
        )

    for p in range(problems):

        @pl.when(winner[p] == place[0])
        def _(p=p):
            window_copy(p).start()

    for p in range(problems):

        @pl.when(winner[p] == place[0])
        def _(p=p):
            window_copy(p).wait()

    rows = lax.broadcasted_iota(jnp.int32, (16, 128), 0)
    for j in range(problems):
        p = j ^ (place[1] * half + place[3] * (half // 2))
        _, offset = start_of(p)
        mine = winner[p] == place[0]
        where = (keep if j < half else send, j % half)
        for kv in range(2):
            head = jnp.where(
                rows < offset,
                window[p, kv, 64:80, :].astype(jnp.float32),
                window[p, kv, 0:16, :].astype(jnp.float32),
            )
            head = jnp.where(mine, head, 0.0).astype(jnp.bfloat16)
            tail = window[p, kv, 16:64, :].astype(jnp.float32)
            tail = jnp.where(mine, tail, 0.0).astype(jnp.bfloat16)
            base = where[1] * BLOCK
            where[0][kv, base : base + 16, :] = head
            where[0][kv, base + 16 : base + BLOCK, :] = tail


def old_kernel(
    lengths_in, queries_in, fresh_in, cache, out, peak, total, passed, lengths, fresh, held, sems, *, first, factor
):
    problems = out.shape[0]
    group = passed.shape[1] // 2
    copies = [
        pltpu.make_async_copy(lengths_in, lengths, sems.at[problems]),
        pltpu.make_async_copy(queries_in.at[first : first + problems], passed, sems.at[problems + 1]),
        pltpu.make_async_copy(fresh_in.at[first : first + problems], fresh, sems.at[problems + 2]),
    ]
    for copy in copies:
        copy.start()
    for i in range(problems):
        copies.append(pltpu.make_async_copy(cache.at[first + i, 0], held.at[i], sems.at[i]))
        copies[-1].start()
    slots = lax.broadcasted_iota(jnp.int32, (2 * group, cache.shape[3]), 1)
    later = lax.broadcasted_iota(jnp.int32, (2 * group, 1), 0) >= group
    for copy in copies:
        copy.wait()
    for i in range(problems):
        query = passed[i]
        wide = query.astype(jnp.float32)
        keys = [fresh[i, 2 * u : 2 * u + 1, :].astype(jnp.float32) for u in range(2)]
        values = [fresh[i, 2 * u + 1 : 2 * u + 2, :].astype(jnp.float32) for u in range(2)]
        new = [jnp.sum(wide * key, -1, keepdims=True) * factor for key in keys]
        new[1] = jnp.where(later, new[1], -jnp.inf)
        scores = lax.dot_general(query, held[i, 0], NT, preferred_element_type=jnp.float32) * factor
        scores = jnp.where(slots < lengths[first + i] - BLOCK, scores, -jnp.inf)
        top = jnp.maximum(jnp.max(scores, -1, keepdims=True), jnp.maximum(new[0], new[1]))
        weights = jnp.exp(scores - top)
        sums = jnp.sum(weights, -1, keepdims=True)
        mixed = jnp.dot(weights.astype(jnp.bfloat16), held[i, 1], preferred_element_type=jnp.float32)
        for u in range(2):
            weight = jnp.exp(new[u] - top)
            sums = sums + weight
            mixed = mixed + weight * values[u]
        out[i] = mixed
        peak[i] = jnp.broadcast_to(top, mixed.shape)
        total[i] = jnp.broadcast_to(sums, mixed.shape)


def fetch_kernel(place, far, near, sems, *, own):
    rows = far.shape[0] // sems.shape[0]
    half = place[2] if own else 1 - place[2]
    columns = pl.ds(pl.multiple_of(half * near.shape[1], 128), near.shape[1])
    copies = [
        pltpu.make_async_copy(far.at[pl.ds(i * rows, rows), columns], near.at[pl.ds(i * rows, rows)], sems.at[i])
        for i in range(sems.shape[0])
    ]
    for copy in copies:
        copy.start()
    for copy in copies:
        copy.wait()


def project(attended, scales, weights, base, out):
    blocks, side = scales.shape[0], weights.shape[0] // scales.shape[0]
    parts = [attended[pl.ds(b, 16, stride=blocks), :].astype(jnp.bfloat16) for b in range(blocks)]
    for c in range(out.shape[1] // CHUNK):
        columns = slice(c * CHUNK, (c + 1) * CHUNK)
        terms = [
            jnp.dot(parts[b], weights[b * side : (b + 1) * side, columns], preferred_element_type=jnp.float32)
            for b in range(blocks)
        ]
        for n in range(CHUNK // 128):
            block = base // 128 + c * (CHUNK // 128) + n
            sums = terms[0][:, n * 128 : (n + 1) * 128] * scales[0, block]
            for b in range(1, blocks):
                sums = sums + terms[b][:, n * 128 : (n + 1) * 128] * scales[b, block]
            out[:, c * CHUNK + n * 128 : c * CHUNK + (n + 1) * 128] = sums.astype(out.dtype)


def fork_kernel(place, mine, other, *refs, factor):
    parts, (scales_in, weights, attended, out, scales, sem) = refs[:8], refs[8:]
    scales_copy = pltpu.make_async_copy(scales_in, scales, sem)
    scales_copy.start()
    old, peak, total, queries = (jnp.concatenate([parts[i][...], parts[i + 4][...]], 0) for i in range(4))
    rows, keys_here = queries.shape[0], mine.shape[1]
    per_row = rows // (2 * keys_here // BLOCK)
    halves = []
    for half, ref in ((place[1], mine), (1 - place[1], other)):
        scores = lax.dot_general(queries, ref[0], NT, preferred_element_type=jnp.float32) * factor
        row = lax.broadcasted_iota(jnp.int32, scores.shape, 0) // per_row
        owner = lax.broadcasted_iota(jnp.int32, scores.shape, 1) // BLOCK
        owner = (owner ^ (place[3] * (keys_here // BLOCK // 2))) + half * (keys_here // BLOCK)
        halves.append(jnp.where(row == owner, scores, -jnp.inf))
    top = jnp.maximum(jnp.max(halves[0], -1, keepdims=True), jnp.max(halves[1], -1, keepdims=True))
    top = jnp.maximum(peak, top)
    kept = jnp.exp(peak - top)
    sums = total * kept
    mixed = old * kept
    for scores, ref in zip(halves, (mine, other)):
        share = jnp.exp(scores - top[:, :1])
        sums = sums + jnp.sum(share, -1, keepdims=True)
        mixed = mixed + jnp.dot(share.astype(jnp.bfloat16), ref[1], preferred_element_type=jnp.float32)
    attended[...] = (mixed / sums).astype(jnp.bfloat16).astype(jnp.float32)
    scales_copy.wait()
    project(attended, scales, weights, (1 - place[2]) * out.shape[1], out)


def project_kernel(place, attended, scales_in, weights, out, scales, sem):
    scales_copy = pltpu.make_async_copy(scales_in, scales, sem)
    scales_copy.start()
    scales_copy.wait()
    project(attended, scales, weights, place[2] * out.shape[1], out)


def params(mib, flops, size):
    return dict(
        compiler_params=pltpu.CompilerParams(vmem_limit_bytes=mib * 2**20),
        cost_estimate=pl.CostEstimate(flops=flops, bytes_accessed=size, transcendentals=0),
    )


def local(hidden_in, queries, new_kv, kv_cache, lengths, winner, out_values, out_scales):
    problems, _, _, slots, head_dim = kv_cache.shape
    steps, heads = queries.shape[1], queries.shape[2]
    width = out_values.shape[1]
    factor = 1.0 / math.sqrt(head_dim)
    cand, tp = lax.axis_index("cand"), lax.axis_index("tp")
    far_cache, far_lengths, winner, far_values, far_scales = (
        pltpu.with_memory_space_constraint(x, pltpu.HBM) for x in (kv_cache, lengths, winner, out_values, out_scales)
    )
    place = jnp.stack([cand, cand % 2, tp % 2, (cand // 8 + cand // 16) % 2]).astype(jnp.int32)
    half = width // 2
    bf16, f32 = jnp.bfloat16, jnp.float32

    fork_shape = jax.ShapeDtypeStruct((2, problems // 2 * BLOCK, head_dim), bf16)
    keep, send = pl.pallas_call(
        extract_kernel,
        out_shape=(fork_shape, fork_shape),
        in_specs=[SMEM, HBM, HBM, HBM],
        out_specs=(VMEM, VMEM),
        scratch_shapes=[
            pltpu.SMEM((problems,), jnp.int32),
            pltpu.SMEM((problems,), jnp.int32),
            pltpu.VMEM((problems, 2, WINDOW, head_dim), bf16),
            pltpu.SemaphoreType.DMA((problems + 2,)),
        ],
        **params(4, 0, 2**19),
    )(place, far_lengths, winner, far_cache)

    def attend_old(queries, fresh, lengths, first):
        queries, fresh, lengths = (
            pltpu.with_memory_space_constraint(x, pltpu.HBM) for x in (queries, fresh, lengths)
        )
        partial = jax.ShapeDtypeStruct((problems // 2, steps * heads, head_dim), f32)
        return pl.pallas_call(
            functools.partial(old_kernel, first=first, factor=factor),
            out_shape=(partial,) * 3 + (jax.ShapeDtypeStruct(partial.shape, bf16),),
            in_specs=[HBM, HBM, HBM, HBM],
            out_specs=(VMEM,) * 4,
            scratch_shapes=[
                pltpu.SMEM(lengths.shape, jnp.int32),
                pltpu.VMEM((problems // 2, *fresh.shape[1:]), bf16),
                pltpu.VMEM((problems // 2, 2, slots, head_dim), bf16),
                pltpu.SemaphoreType.DMA((problems // 2 + 3,)),
            ],
            **params(8, 2**23, 2**20),
        )(lengths, queries, fresh, far_cache)

    def fetch_weights(weights, own):
        return pl.pallas_call(
            functools.partial(fetch_kernel, own=own),
            out_shape=jax.ShapeDtypeStruct((weights.shape[0], half), bf16),
            in_specs=[SMEM, HBM],
            out_specs=VMEM,
            scratch_shapes=[pltpu.SemaphoreType.DMA((8,))],
            **params(8, 0, 2**23),
        )(place, weights)

    block = keep + exchange(send, "cand", 32, 1)
    queries = queries.reshape(problems, steps * heads, head_dim)
    fresh = new_kv.reshape(problems, 2 * steps, head_dim)
    middle = block.shape[1] // 2
    far_values, block = lax.optimization_barrier((far_values, block))
    received, home_weights = lax.optimization_barrier(
        (exchange(block[:, middle:], "cand", 32, 8), fetch_weights(far_values, True))
    )
    block = block[:, :middle] + received
    queries, fresh, lengths, block = lax.optimization_barrier((queries, fresh, lengths, block))
    received, part = lax.optimization_barrier(
        (exchange(block, "cand", 32, 24), attend_old(queries, fresh, lengths, 0))
    )
    block = block + received
    queries, fresh, lengths, block = lax.optimization_barrier((queries, fresh, lengths, block))
    received, rest = lax.optimization_barrier(
        (exchange(block, "cand", 32, 2), attend_old(queries, fresh, lengths, problems // 2))
    )
    block = block + received
    far_values, block = lax.optimization_barrier((far_values, block))
    received, away_weights = lax.optimization_barrier(
        (exchange(block, "cand", 32, 6), fetch_weights(far_values, False))
    )
    block = block + received
    received = exchange(block, "cand", 32, 8)
    block = jnp.concatenate([block, received], axis=1)
    other = exchange(block, "cand", 32, 1)

    away_weights, home_weights = (
        pltpu.with_memory_space_constraint(x, pltpu.VMEM) for x in (away_weights, home_weights)
    )
    flat = (problems * steps * heads, head_dim)
    half_shape = jax.ShapeDtypeStruct((problems * steps, half), bf16)
    scratch = [pltpu.SMEM(out_scales.shape, f32), pltpu.SemaphoreType.DMA]
    attended, away = pl.pallas_call(
        functools.partial(fork_kernel, factor=factor),
        out_shape=(jax.ShapeDtypeStruct(flat, f32), half_shape),
        in_specs=[SMEM] + [VMEM] * 10 + [HBM, VMEM],
        out_specs=(VMEM, VMEM),
        scratch_shapes=scratch,
        **params(14, 2**26, 2**22),
    )(
        place,
        block,
        other,
        *(x.reshape(flat[0] // 2, head_dim) for x in (*part, *rest)),
        far_scales,
        away_weights,
    )
    arrived = exchange(away, "tp", 8, 1)
    home = pl.pallas_call(
        project_kernel,
        out_shape=half_shape,
        in_specs=[SMEM, VMEM, HBM, VMEM],
        out_specs=VMEM,
        scratch_shapes=scratch,
        **params(14, 2**26, 2**22),
    )(place, attended, far_scales, home_weights)

    sums = home + arrived
    ahead, back, across = (exchange(sums, "tp", 8, bit) for bit in (2, 6, 4))
    residual = hidden_in.reshape(problems * steps, width)
    residual = lax.dynamic_slice_in_dim(residual, (tp % 2) * half, half, 1)
    pairs = (sums.astype(f32) + ahead.astype(f32)) + (back.astype(f32) + across.astype(f32))
    mixed = (residual.astype(f32) + pairs).astype(bf16)
    neighbour = exchange(mixed, "tp", 8, 1)
    first = tp % 2 == 0
    result = jnp.concatenate(
        [jnp.where(first, mixed, neighbour), jnp.where(first, neighbour, mixed)], axis=1
    )
    return result.reshape(hidden_in.shape)


def solution(mesh):
    placed = (
        P("cand", None, None),
        P("cand", None, "tp", None),
        P("cand", None, "tp", None, None),
        P("cand", "tp", None, None, None),
        P("cand"),
        P(),
        P("tp", None),
        P("tp", None),
    )
    return jax.shard_map(
        local, mesh=mesh, in_specs=placed, out_specs=P("cand", None, None), check_vma=False
    )
```
